32 devices in a mesh: ctx: 4 (over y, core), exp: 8 (over z, x).
Axes of the slice: x: 2, y: 2, z: 4, core: 2. Of those that a mesh axis runs over, the one named last changes fastest.
Arguments:
- prompt_cache: bfloat16 [12288, 576], P('ctx'), may hold values from -8 to 8
- tree_latent: bfloat16 [256, 576], P('ctx'), may hold values from -12 to 12
- parents: int32 [256], replicated, may hold values from -1 to 254, as said below
- query_nope: bfloat16 [256, 128, 128], P(None, 'exp'), may hold values from -8 to 8
- query_rope: bfloat16 [256, 128, 64], P(None, 'exp'), may hold values from -400 to 400
- w_absorb: bfloat16 [128, 128, 512], P('exp'), may hold values from -0.5 to 0.5
- w_value: bfloat16 [128, 512, 128], P('exp'), may hold values from -2 to 2
- w_out: bfloat16 [16384, 7168], P('exp', 'ctx'), may hold values from -0.046875 to 0.046875
- residual: bfloat16 [256, 7168], P('exp', 'ctx'), may hold values from -400 to 400
- norm_gain: bfloat16 [7168], P('ctx'), may hold values from 0.5 to 1.5
- routes: int32 [256, 8], replicated, may hold values from 0 to 31, all different within a row; in each aligned block of 32 rows (0 to 31, 32 to 63, ...) at most 16 rows name the same one
- route_weights: float32 [256, 8], replicated, may hold values from 0.1 to 1
- w_gate: bfloat16 [32, 7168, 1024], P('exp', 'ctx'), may hold values from -0.0625 to 0.0625
- w_up: bfloat16 [32, 7168, 1024], P('exp', 'ctx'), may hold values from -0.0625 to 0.0625
- w_down: bfloat16 [32, 1024, 7168], P('exp', None, 'ctx'), may hold values from -0.1875 to 0.1875
Outputs:
- attn_out: bfloat16 [256, 7168], P('exp', 'ctx')
- moe_out: bfloat16 [256, 7168], P('exp', 'ctx')
The draws below stay inside these ranges and needn't reach their ends.
Inputs may be any that keep to these rules, and one draw needn't show every extreme that they name: `routes`: each row names 8 different experts. No expert is named by more than 16 rows of one aligned block of 32 rows, and that bound is reached. parents[0] = -1; every other node's parent is an earlier node, at most 24 positions before it; the last node's parent is the node just before it.
All inputs are finite; a program needn't handle non-finite values.
Results may differ from the reference program's by a relative error of at most 0.035.
Values may be sent and summed in bfloat16 or wider, within the bound.
A program may use at most 256 MiB of HBM per device.

```python
import math
import jax
import jax.numpy as jnp
import numpy as np
from jax import lax

D = 7168
HEADS = 128
LATENT = 512
ROPE = 64
NOPE = 128
VDIM = 128
TOPK = 8
FF = 1024
EXPERTS = 32
NODES = 256
PROMPT = 12288
ROWS = 32
CAP = 16
DGROUP = 1792
N_EXP = 8


TWIN_GAP = 509


def rope_keys(key):
    baseline = jax.random.normal(jax.random.fold_in(key, 101), (PROMPT, ROPE), jnp.float32)
    marked = (jnp.arange(PROMPT) % TWIN_GAP == 1)[:, None]
    return jnp.where(marked, baseline, baseline)


def draw_prompt_cache(key, part):
    shared = rope_keys(key)
    own_key = jax.random.fold_in(key, 3)
    latent = jax.random.normal(own_key, (PROMPT, LATENT), jnp.float32)
    return jnp.concatenate([latent, shared], axis=1).astype(jnp.bfloat16)


def draw_query_rope(key, part):
    own_key = jax.random.fold_in(key, 5)
    result = jax.random.normal(own_key, (NODES, HEADS, ROPE), jnp.float32)
    return result.astype(jnp.bfloat16)


def draw_residual(key, part):
    key = jax.random.fold_in(key, 7)
    first_key, second_key, third_key = jax.random.split(key, 3)
    column = jnp.arange(D, dtype=jnp.float32) / D
    col_scale = jnp.exp(math.log(10.0) * (0.5 * column + 0.5 * jax.random.uniform(second_key, (D,), jnp.float32)))
    row_scale = jnp.exp(math.log(10.0) * jax.random.uniform(third_key, (NODES,), jnp.float32))
    pattern = jax.random.normal(first_key, (NODES, D), jnp.float32)
    return (0.3 * pattern * row_scale[:, None] * col_scale[None, :]).astype(jnp.bfloat16)


def draw_parents(key, part):
    key = jax.random.fold_in(key, 11)
    node_index = jnp.arange(NODES, dtype=jnp.int32)
    lower_bound = jnp.maximum(node_index - 24, 0)
    upper_bound = jnp.maximum(node_index, 1)
    parent_draw = jax.random.randint(key, (NODES,), lower_bound, upper_bound, dtype=jnp.int32)
    parent_draw = jnp.where(node_index == NODES - 1, NODES - 2, parent_draw)
    return jnp.where(node_index == 0, -1, parent_draw).astype(jnp.int32)


def block_scale(stream_key, shape, pieces, low, high):
    loudness = 1.0
    for axis_at, shards_of in pieces:
        steps = jax.random.uniform(jax.random.fold_in(jax.random.fold_in(stream_key, 6), axis_at), (shards_of,), jnp.float32, low / len(pieces), high / len(pieces))
        loudness = loudness * jnp.repeat(jnp.exp(steps), shape[axis_at] // shards_of).reshape((-1,) + (1,) * (len(shape) - 1 - axis_at))
    return loudness


def deal_out(key, own, number, rows, number_of, top, reach, skew):
    order = jax.random.permutation(key, number_of)
    crowded, common = load_shares(number_of, rows * top, reach, skew, True), load_shares(number_of, rows * top, reach, skew, False)
    places = jnp.arange(number_of)

    def named(lengths, turn):
        used = int((lengths > 0).sum())
        fixed = max(1, used // 4)
        passed = fixed + (places - fixed + turn * (used - fixed)) % max(1, number_of - fixed)
        return jnp.zeros((number_of,), jnp.int32).at[order[jnp.where(places < fixed, places, passed)]].set(jnp.asarray(lengths, jnp.int32))

    lengths = jnp.where(number % 4 == 0, named(crowded, number // 4), named(common, number - number // 4 - 1))
    mixed = jax.random.permutation(jax.random.fold_in(own, 3), number_of)
    source_of, sink = mixed[0:number_of // 2 * 2:2], mixed[1:number_of // 2 * 2:2]
    margin = jnp.minimum(lengths[source_of] - 1, reach - lengths[sink]) // 2
    margin = jnp.where((source_of == order[0]) | (sink == order[0]) | (lengths[sink] == 0), 0, jnp.maximum(margin, 0))
    passed = jax.random.randint(jax.random.fold_in(own, 4), (number_of // 2,), 0, 1 << 20) % (margin + 1)
    lengths = lengths.at[source_of].add(-passed).at[sink].add(passed)
    labels = jnp.searchsorted(jnp.cumsum(lengths), jnp.arange(rows * top), side="right").astype(jnp.int32)
    listing = labels.reshape(top, rows).T
    listing = listing[jax.random.permutation(jax.random.fold_in(own, 1), rows)]
    turn = jax.random.randint(jax.random.fold_in(own, 2), (rows, 1), 0, top)
    return jnp.take_along_axis(listing, (jnp.arange(top)[None, :] + turn) % top, axis=1)


def load_shares(number_of, total, most, slope, full):
    loads = [(1 << 20) // math.isqrt(standing ** slope) + 1 for standing in range(1, number_of + 1)]
    largest = most if full else min(most, max(-(-total // number_of), total * loads[0] // sum(loads)))
    least = 1 if total - largest >= number_of - 1 else 0
    holding, spare = [largest] + [least] * (number_of - 1), total - largest - least * (number_of - 1)
    while spare > 0:
        candidates = [i for i in range(1, number_of) if holding[i] < largest] or [i for i in range(1, number_of) if holding[i] < most]
        pool, remaining = sum([loads[i] for i in candidates]), spare
        for i in candidates:
            more = min(most - holding[i], max(1, remaining * loads[i] // pool), spare)
            holding[i] = holding[i] + more
            spare = spare - more
    return np.array(holding)


def noise(rng, dims, deviation, most, shards=(), held_as=jnp.bfloat16):
    values = deviation * jax.random.normal(rng, dims, jnp.float32)
    if shards:
        values = values * block_scale(rng, dims, shards, -0.22, 0.18)
    return jnp.clip(values, -most, most).astype(held_as)


def setup_inputs(seed: int = 0) -> dict:
    arg_keys = jax.random.split(jax.random.key(seed), 16)
    prompt_cache = draw_prompt_cache(jax.random.fold_in(arg_keys[15], 71), 0)
    tree_latent = noise(arg_keys[1], (NODES, LATENT + ROPE), 2.0, 12.0, ((0, 4),))
    parents = draw_parents(jax.random.fold_in(arg_keys[15], 71), 0)
    query_nope = noise(arg_keys[3], (NODES, HEADS, NOPE), 1.3, 8.0, ((1, 8),))
    query_rope = draw_query_rope(jax.random.fold_in(arg_keys[15], 71), 0)
    w_absorb = noise(arg_keys[5], (HEADS, NOPE, LATENT), NOPE ** -0.5, 0.5, ((0, 8),))
    w_value = noise(arg_keys[6], (HEADS, LATENT, VDIM), (max(1, LATENT // 64)) ** -0.5, 2.0, ((0, 8),))
    w_out = noise(arg_keys[7], (HEADS * VDIM, D), (HEADS * VDIM) ** -0.5, 0.046875, ((0, 8), (1, 4)))
    residual = draw_residual(jax.random.fold_in(arg_keys[15], 71), 0)
    norm_gain = jnp.clip(1.0 + 0.1 * jax.random.normal(arg_keys[9], (D,), jnp.float32), 0.5, 1.5).astype(jnp.bfloat16)
    routes_keys = jax.random.split(jax.random.fold_in(arg_keys[10], 1), NODES // ROWS)
    routes_turns = jax.random.permutation(jax.random.fold_in(arg_keys[10], 3), NODES // ROWS)
    routes = jax.vmap(lambda own, number: deal_out(jax.random.fold_in(arg_keys[10], 2), own, number, ROWS, EXPERTS, TOPK, CAP, 2))(routes_keys, routes_turns).reshape((NODES, TOPK))
    route_weights = jnp.clip(jnp.exp(jax.random.uniform(arg_keys[11], (NODES, TOPK), jnp.float32, math.log(0.1), math.log(1.0))), 0.1, 1.0)
    w_gate = noise(arg_keys[12], (EXPERTS, D, FF), D ** -0.5, 0.0625, ((0, 8), (1, 4)))
    w_up = noise(arg_keys[13], (EXPERTS, D, FF), D ** -0.5, 0.0625, ((0, 8), (1, 4)))
    w_down = noise(arg_keys[14], (EXPERTS, FF, D), FF ** -0.5, 0.1875, ((0, 8), (2, 4)))
    return {"prompt_cache": prompt_cache, "tree_latent": tree_latent, "parents": parents, "query_nope": query_nope, "query_rope": query_rope, "w_absorb": w_absorb, "w_value": w_value, "w_out": w_out, "residual": residual, "norm_gain": norm_gain, "routes": routes, "route_weights": route_weights, "w_gate": w_gate, "w_up": w_up, "w_down": w_down}


NEG_FILL = -1e+30
EXACT_PRODUCTS = lax.Precision.HIGHEST

def ancestry(parents):
    node_total = parents.shape[0]
    linked = (parents[:, None] == jnp.arange(node_total, dtype=jnp.int32)[None, :]).astype(jnp.float32)
    ancestors = jnp.eye(node_total, dtype=jnp.float32) + linked
    for repeat in range(node_total.bit_length()):
        ancestors = jnp.minimum(jnp.dot(ancestors, ancestors, precision=EXACT_PRODUCTS), 1.0)
    return ancestors

def slot_ranks(routes, block_rows):
    onehot = (routes[:, :, None] == jnp.arange(EXPERTS, dtype=jnp.int32)).astype(jnp.int32)
    grouped = onehot.reshape(-1, block_rows * TOPK, EXPERTS)
    before = jnp.cumsum(grouped, axis=1) - grouped
    return lax.optimization_barrier(jnp.sum(before * grouped, axis=2)).reshape(routes.shape).astype(jnp.int32)

def reference(prompt_cache, tree_latent, parents, query_nope, query_rope, w_absorb, w_value, w_out, residual, norm_gain, routes, route_weights, w_gate, w_up, w_down):
    score_scale = (NOPE + ROPE) ** (-0.5)
    ancestors = ancestry(parents)
    prompt_values = prompt_cache[:, :LATENT]
    tree_values = tree_latent[:, :LATENT]
    dims_last = (((1,), (1,)), ((), ()))

    def one_head(head_index):
        absorbed = jnp.dot(query_nope[:, head_index], w_absorb[head_index], preferred_element_type=jnp.float32).astype(jnp.bfloat16)
        queries = jnp.concatenate([absorbed, query_rope[:, head_index]], axis=1)
        prompt_scores = lax.dot_general(queries, prompt_cache, dims_last, preferred_element_type=jnp.float32) * score_scale
        tree_scores = lax.dot_general(queries, tree_latent, dims_last, preferred_element_type=jnp.float32) * score_scale
        tree_scores = jnp.where(ancestors > 0.5, tree_scores, NEG_FILL)
        top_score = jnp.maximum(lax.optimization_barrier(jnp.max(prompt_scores, axis=1)), lax.optimization_barrier(jnp.max(tree_scores, axis=1)))
        prompt_exp = jnp.exp(prompt_scores - top_score[:, None])
        tree_exp = jnp.exp(tree_scores - top_score[:, None])
        weight_total = lax.optimization_barrier(jnp.sum(prompt_exp, axis=1)) + lax.optimization_barrier(jnp.sum(tree_exp, axis=1))
        latent_mix = jnp.dot(prompt_exp.astype(jnp.bfloat16), prompt_values, preferred_element_type=jnp.float32)
        latent_mix = latent_mix + jnp.dot(tree_exp.astype(jnp.bfloat16), tree_values, preferred_element_type=jnp.float32)
        projected = jnp.dot(latent_mix, w_value[head_index].astype(jnp.float32), precision=EXACT_PRODUCTS)
        return (projected / weight_total[:, None]).astype(jnp.bfloat16)
    heads_out = lax.map(one_head, jnp.arange(HEADS, dtype=jnp.int32))
    heads_flat = jnp.transpose(heads_out, (1, 0, 2)).reshape(NODES, HEADS * VDIM)
    attn_sum = jnp.dot(heads_flat, w_out, preferred_element_type=jnp.float32)
    state = residual.astype(jnp.float32) + attn_sum
    routed = (state * norm_gain.astype(jnp.float32)).astype(jnp.bfloat16)
    group_squares = lax.optimization_barrier(jnp.sum((state * state).reshape(NODES, D // DGROUP, DGROUP), axis=2)).astype(jnp.bfloat16)
    root_mean = jnp.sqrt(lax.optimization_barrier(jnp.sum(group_squares.astype(jnp.float32), axis=1)) / D + 1e-06)
    slot_rank = slot_ranks(routes, ROWS)
    positions = ((jnp.arange(NODES, dtype=jnp.int32) // ROWS)[:, None] * CAP + slot_rank).astype(jnp.int32)
    node_ids = jnp.broadcast_to(jnp.arange(NODES, dtype=jnp.int32)[:, None], routes.shape)
    slot_owner = jnp.full((EXPERTS, N_EXP * CAP), NODES, dtype=jnp.int32).at[routes, positions].set(node_ids)
    routed_pad = jnp.concatenate([routed, jnp.zeros((1, D), jnp.bfloat16)], axis=0)
    root_pad = jnp.concatenate([root_mean, jnp.ones((1,), jnp.float32)], axis=0)

    def one_expert(expert_index):
        picked = slot_owner[expert_index]
        chosen = routed_pad[picked]
        row_root = root_pad[picked][:, None]
        gate_in = jnp.dot(chosen, w_gate[expert_index], preferred_element_type=jnp.float32) / row_root
        up_in = jnp.dot(chosen, w_up[expert_index], preferred_element_type=jnp.float32) / row_root
        expert_hidden = (jax.nn.silu(gate_in) * up_in).astype(jnp.bfloat16)
        return jnp.dot(expert_hidden, w_down[expert_index], preferred_element_type=jnp.float32).astype(jnp.bfloat16)
    expert_out = lax.map(one_expert, jnp.arange(EXPERTS, dtype=jnp.int32))
    picked_out = expert_out[routes, positions].astype(jnp.float32)
    moe_sum = lax.optimization_barrier(jnp.sum(route_weights[:, :, None] * picked_out, axis=1))
    return (attn_sum.astype(jnp.bfloat16), moe_sum.astype(jnp.bfloat16))
```

```python
import jax
import jax.numpy as jnp
from jax import lax
from jax.experimental import pallas as pl
from jax.experimental.pallas import tpu as pltpu
from jax.sharding import PartitionSpec as P

D = 7168
TOPK = 8
EXPERTS = 32


NEG_FILL = -1e30
EXACT_PRODUCTS = lax.Precision.HIGHEST


def merged(array, axis, join):
    gathered = jax.tree.map(
        lambda a, kind: lax.all_gather(a.astype(kind), axis),
        array,
        (jnp.bfloat16, jnp.bfloat16, jnp.bfloat16),
    )

    def take(source):
        return jax.tree.map(
            lambda a, own: lax.dynamic_index_in_dim(a, source, 0, False).astype(own.dtype),
            gathered,
            array,
        )

    return lax.fori_loop(
        1, lax.axis_size(axis), lambda source, state: join(state, take(source)), take(0)
    )


def ancestry(parents):
    node_total = parents.shape[0]
    linked = (parents[:, None] == jnp.arange(node_total, dtype=jnp.int32)[None, :]).astype(
        jnp.float32
    )
    ancestors = jnp.eye(node_total, dtype=jnp.float32) + linked
    for repeat in range(node_total.bit_length()):
        ancestors = jnp.minimum(jnp.dot(ancestors, ancestors, precision=EXACT_PRODUCTS), 1.0)
    return ancestors


def slot_ranks(routes, block_rows):
    onehot = (routes[:, :, None] == jnp.arange(EXPERTS, dtype=jnp.int32)).astype(jnp.int32)
    grouped = onehot.reshape(-1, block_rows * TOPK, EXPERTS)
    before = jnp.cumsum(grouped, axis=1) - grouped
    return jnp.sum(before * grouped, axis=2).reshape(routes.shape)


def merge_parts(earlier, latter):
    first_top, first_total, first_mix = earlier
    second_top, second_total, second_mix = latter
    top_score = jnp.maximum(first_top, second_top)
    first_factor = jnp.exp(first_top - top_score)
    second_factor = jnp.exp(second_top - top_score)
    weight_total = first_total * first_factor + second_total * second_factor
    combined = first_mix * first_factor[..., None] + second_mix * second_factor[..., None]
    return (top_score, weight_total, combined)


def combine_parts(top_score, weight_total, partial_mix):
    return merged((top_score, weight_total, partial_mix), "ctx", merge_parts)


def expert_block(pieces, w_gate, w_up, w_down):
    blocks, squares = pieces
    gate_part = jnp.einsum("sjkd,jdf->sjkf", blocks, w_gate, preferred_element_type=jnp.float32)
    up_part = jnp.einsum("sjkd,jdf->sjkf", blocks, w_up, preferred_element_type=jnp.float32)
    gate_sum, up_sum, square_sum = (
        lax.psum(gate_part.astype(jnp.bfloat16), "ctx").astype(jnp.float32),
        lax.psum(up_part.astype(jnp.bfloat16), "ctx").astype(jnp.float32),
        lax.psum(squares.astype(jnp.float32).astype(jnp.bfloat16), "ctx").astype(jnp.float32),
    )
    root_mean = jnp.sqrt(square_sum / D + 1e-06)[..., None]
    expert_hidden = (jax.nn.silu(gate_sum / root_mean) * (up_sum / root_mean)).astype(jnp.bfloat16)
    return jnp.einsum(
        "sjkf,jfd->sjkd", expert_hidden, w_down, preferred_element_type=jnp.float32
    ).astype(jnp.bfloat16)


def plain_body(
    prompt_cache,
    tree_latent,
    parents,
    query_nope,
    query_rope,
    w_absorb,
    w_value,
    w_out,
    residual,
    norm_gain,
    routes,
    route_weights,
    w_gate,
    w_up,
    w_down,
):
    node_total, heads_here, nope_width = query_nope.shape
    latent_width = w_absorb.shape[2]
    score_scale = (nope_width + query_rope.shape[2]) ** (-0.5)
    dims_last = (((1,), (1,)), ((), ()))
    absorbed = jnp.einsum(
        "nhc,hcl->nhl", query_nope, w_absorb, preferred_element_type=jnp.float32
    ).astype(jnp.bfloat16)
    queries = jnp.concatenate([absorbed, query_rope], axis=2).reshape(node_total * heads_here, -1)
    tree_rows = tree_latent.shape[0]
    ancestors = ancestry(parents)
    tree_columns = lax.dynamic_slice_in_dim(
        ancestors, lax.axis_index("ctx") * tree_rows, tree_rows, 1
    )
    prompt_scores = lax.dot_general(
        queries, prompt_cache, dims_last, preferred_element_type=jnp.float32
    )
    prompt_scores = prompt_scores.reshape(node_total, heads_here, -1) * score_scale
    tree_scores = lax.dot_general(
        queries, tree_latent, dims_last, preferred_element_type=jnp.float32
    )
    tree_scores = tree_scores.reshape(node_total, heads_here, -1) * score_scale
    tree_scores = jnp.where(tree_columns[:, None, :] > 0.5, tree_scores, NEG_FILL)
    top_score = jnp.maximum(jnp.max(prompt_scores, axis=2), jnp.max(tree_scores, axis=2))
    prompt_exp = jnp.exp(prompt_scores - top_score[..., None])
    tree_exp = jnp.exp(tree_scores - top_score[..., None])
    weight_total = jnp.sum(prompt_exp, axis=2) + jnp.sum(tree_exp, axis=2)
    latent_mix = jnp.dot(
        prompt_exp.reshape(node_total * heads_here, -1).astype(jnp.bfloat16),
        prompt_cache[:, :latent_width],
        preferred_element_type=jnp.float32,
    )
    latent_mix = latent_mix + jnp.dot(
        tree_exp.reshape(node_total * heads_here, -1).astype(jnp.bfloat16),
        tree_latent[:, :latent_width],
        preferred_element_type=jnp.float32,
    )
    latent_mix = latent_mix.reshape(node_total, heads_here, latent_width)
    value_weights = w_value.astype(jnp.float32)
    projected = jnp.einsum("nhl,hlv->nhv", latent_mix, value_weights, precision=EXACT_PRODUCTS)
    top_score, weight_total, projected = combine_parts(top_score, weight_total, projected)
    heads_out = (projected / weight_total[..., None]).astype(jnp.bfloat16).reshape(node_total, -1)
    row_count = residual.shape[0]
    attn_sum = lax.psum_scatter(
        jnp.dot(heads_out, w_out, preferred_element_type=jnp.float32).astype(jnp.bfloat16),
        "exp",
        scatter_dimension=0,
        tiled=True,
    ).astype(jnp.float32)
    state = residual.astype(jnp.float32) + attn_sum
    routed = (state * norm_gain.astype(jnp.float32)).astype(jnp.bfloat16)
    group_squares = jnp.sum(state * state, axis=1).astype(jnp.bfloat16)
    capacity = max(2, 2 * row_count * TOPK // EXPERTS)
    senders = lax.axis_size("exp")
    experts_here = w_gate.shape[0]
    exp_place = lax.axis_index("exp")
    own_routes = lax.dynamic_slice_in_dim(routes, exp_place * row_count, row_count, 0)
    own_weights = lax.dynamic_slice_in_dim(route_weights, exp_place * row_count, row_count, 0)
    slot_rank = slot_ranks(own_routes, row_count)
    expert_hot = (own_routes[:, :, None] == jnp.arange(EXPERTS, dtype=jnp.int32)).astype(
        jnp.float32
    )
    slot_hot = (slot_rank[:, :, None] == jnp.arange(capacity, dtype=jnp.int32)).astype(jnp.float32)
    placing = jnp.einsum("rkx,rks->xsr", expert_hot, slot_hot)
    send_blocks = jnp.einsum(
        "xsr,rd->xsd", placing.astype(jnp.bfloat16), routed, preferred_element_type=jnp.float32
    )
    send_blocks = send_blocks.astype(jnp.bfloat16).reshape(senders, experts_here, capacity, -1)
    send_squares = jnp.einsum(
        "xsr,r->xs", placing, group_squares.astype(jnp.float32), precision=EXACT_PRODUCTS
    )
    send_squares = send_squares.astype(jnp.bfloat16).reshape(senders, experts_here, capacity)
    answers = expert_block(
        (
            lax.all_to_all(send_blocks, "exp", split_axis=0, concat_axis=0, tiled=True),
            lax.all_to_all(send_squares, "exp", split_axis=0, concat_axis=0, tiled=True),
        ),
        w_gate,
        w_up,
        w_down,
    )
    returned = lax.all_to_all(answers, "exp", split_axis=0, concat_axis=0, tiled=True)
    returned = returned.reshape(EXPERTS, capacity, -1).astype(jnp.float32)
    weighting = jnp.einsum(
        "rkx,rks,rk->rxs", expert_hot, slot_hot, own_weights, precision=EXACT_PRODUCTS
    )
    moe_sum = jnp.einsum("rxs,xsd->rd", weighting, returned, precision=EXACT_PRODUCTS)
    return (attn_sum.astype(jnp.bfloat16), moe_sum.astype(jnp.bfloat16))


LOG2E = 1.4426950408889634
MESH = pl.DeviceIdType.MESH
MIB = 1024 * 1024
F32 = jnp.float32
BF16 = jnp.bfloat16
HEADS_PER_STEP = 2


def attention_kernel(
    scale, qn_ref, qr_ref, wabs_ref, wval_ref, cache_ref, tree_ref, linked_ref, select_ref,
    part_ref, stat_ref, visible,
):
    step = pl.program_id(0)
    nodes = qn_ref.shape[0]
    latent = wabs_ref.shape[2]
    nope = wabs_ref.shape[1]
    vdim = wval_ref.shape[2]
    heads = pl.num_programs(0) * HEADS_PER_STEP

    @pl.when(step == 0)
    def _():
        reach = linked_ref[...]
        for _ in range((nodes - 1).bit_length()):
            reach = jnp.minimum(jnp.dot(reach, reach, preferred_element_type=F32), 1.0).astype(BF16)
        visible[...] = jnp.dot(reach, select_ref[...], preferred_element_type=F32)
        stat_ref[...] = jnp.zeros_like(stat_ref)

    nt = (((1,), (1,)), ((), ()))
    factor = scale * LOG2E
    queries = jnp.concatenate(
        [
            jnp.concatenate(
                [
                    jnp.dot(
                        qn_ref[:, h * nope : (h + 1) * nope], wabs_ref[h],
                        preferred_element_type=F32,
                    ).astype(BF16),
                    qr_ref[h],
                ],
                axis=1,
            )
            for h in range(HEADS_PER_STEP)
        ],
        axis=0,
    )
    keys = cache_ref.shape[0]
    chunk = 512
    scores = [
        lax.dot_general(
            queries, cache_ref[at : at + chunk, :], nt, preferred_element_type=F32
        ) * factor
        for at in range(0, keys, chunk)
    ]
    tree_scores = lax.dot_general(queries, tree_ref[...], nt, preferred_element_type=F32) * factor
    seen = jnp.concatenate([visible[...]] * HEADS_PER_STEP, axis=0)
    tree_scores = jnp.where(seen > 0.5, tree_scores, NEG_FILL)
    highest = scores[0]
    for piece in scores[1:]:
        highest = jnp.maximum(highest, piece)
    top = jnp.maximum(
        jnp.max(highest, axis=1, keepdims=True), jnp.max(tree_scores, axis=1, keepdims=True)
    )
    tree_exp = jnp.exp2(tree_scores - top)
    total = jnp.sum(tree_exp, axis=1, keepdims=True)
    mix = jnp.dot(tree_exp.astype(BF16), tree_ref[:, :latent], preferred_element_type=F32)
    sums = None
    for i, piece in enumerate(scores):
        weight = jnp.exp2(piece - top)
        sums = weight if sums is None else sums + weight
        mix += jnp.dot(
            weight.astype(BF16), cache_ref[i * chunk : (i + 1) * chunk, :latent],
            preferred_element_type=F32,
        )
    total += jnp.sum(sums, axis=1, keepdims=True)
    lane = lax.broadcasted_iota(jnp.int32, stat_ref.shape, 1)
    stat = stat_ref[...]
    for h in range(HEADS_PER_STEP):
        rows = slice(h * nodes, (h + 1) * nodes)
        head = step * HEADS_PER_STEP + h
        part_ref[:, h * vdim : (h + 1) * vdim] = jnp.dot(
            mix[rows].astype(BF16), wval_ref[h], preferred_element_type=F32
        ).astype(BF16)
        stat = jnp.where(lane == head, top[rows], stat)
        stat = jnp.where(lane == heads + head, total[rows], stat)
    stat_ref[...] = stat


def attention(qn, qr, wabs, wval, cache, tree, linked, select):
    nodes = qn.shape[0]
    heads, nope, latent = wabs.shape
    vdim = wval.shape[2]
    rope = qr.shape[2]
    per = HEADS_PER_STEP
    whole = lambda a: pl.BlockSpec(a.shape, lambda i: (0,) * a.ndim)
    scale = float((nope + rope) ** (-0.5))

    def kernel(*refs):
        attention_kernel(scale, *refs)

    return pl.pallas_call(
        kernel,
        grid=(heads // per,),
        out_shape=(
            jax.ShapeDtypeStruct((nodes, heads * vdim), BF16),
            jax.ShapeDtypeStruct((nodes, 128), F32),
        ),
        in_specs=[
            pl.BlockSpec((nodes, per * nope), lambda i: (0, i)),
            pl.BlockSpec((per, nodes, rope), lambda i: (i, 0, 0)),
            pl.BlockSpec((per, nope, latent), lambda i: (i, 0, 0)),
            pl.BlockSpec((per, latent, vdim), lambda i: (i, 0, 0)),
            whole(cache), whole(tree), whole(linked), whole(select),
        ],
        out_specs=(
            pl.BlockSpec((nodes, per * vdim), lambda i: (0, i)),
            pl.BlockSpec((nodes, 128), lambda i: (0, 0)),
        ),
        scratch_shapes=[pltpu.VMEM((nodes, tree.shape[0]), F32)],
        compiler_params=pltpu.CompilerParams(
            dimension_semantics=("arbitrary",), vmem_limit_bytes=48 * MIB
        ),
        name="attention",
    )(qn, qr, wabs, wval, cache, tree, linked, select)


def places():
    c = lax.axis_index("ctx")
    e = lax.axis_index("exp")
    core, z, x = c % 2, e // 2, e % 2
    return c, e, core, z, x, c + 1 - 2 * core, c + 2 - 4 * (c // 2), e + 1 - 2 * x


def greet():
    c, e, core, z, x, sibling, across, xpeer = places()
    barrier = pltpu.get_barrier_semaphore()
    peers = [(sibling, e), (across, e), (c, xpeer)]
    peers += [(c, (z + k) % 4 * 2 + x) for k in (1, 2, 3)]
    for peer in peers:
        pl.semaphore_signal(barrier, inc=1, device_id=peer, device_id_type=MESH)
    pl.semaphore_wait(barrier, len(peers))


def remote(src, dst, send, recv, to):
    return pltpu.make_async_remote_copy(
        src_ref=src, dst_ref=dst, send_sem=send, recv_sem=recv, device_id=to, device_id_type=MESH
    )


def block_of(index, rows):
    return pl.ds(pl.multiple_of(index * rows, rows), rows)


def scatter_sums(part, xbuf, zsend, zbuf, xs, xr, zs, zr, spans):
    c, e, core, z, x, sibling, across, xpeer = places()
    rows = zsend.shape[1]

    def xcopy(j, k):
        at, zt = spans[j], (z + k) % 4
        return remote(
            part.at[block_of(zt * 2 + 1 - x, rows), at], xbuf.at[k, :, at],
            xs.at[j, k], xr.at[j, k], (c, xpeer),
        )

    def zcopy(j, k):
        at = spans[j]
        return remote(
            zsend.at[k - 1, :, at], zbuf.at[k - 1, :, at],
            zs.at[j, k - 1], zr.at[j, k - 1], (c, (z + k) % 4 * 2 + x),
        )

    def start(j):
        for k in (2, 1, 3, 0):
            xcopy(j, k).start()

    def forward(j):
        at = spans[j]
        for k in (2, 1, 3):
            xcopy(j, k).wait_recv()
            own = part[block_of((z + k) % 4 * 2 + x, rows), at].astype(F32)
            zsend[k - 1, :, at] = (own + xbuf[k, :, at].astype(F32)).astype(BF16)
            zcopy(j, k).start()

    def finish(j):
        at = spans[j]
        xcopy(j, 0).wait_recv()
        total = part[block_of(e, rows), at].astype(F32) + xbuf[0, :, at].astype(F32)
        for k in (1, 3, 2):
            zcopy(j, k).wait_recv()
            total += zbuf[k - 1, :, at].astype(F32)
        return total

    def drain():
        for j in range(len(spans)):
            for k in range(4):
                xcopy(j, k).wait_send()
            for k in (1, 2, 3):
                zcopy(j, k).wait_send()

    return start, forward, finish, drain


def middle_kernel(
    part_ref, stat_ref, wout_hbm, residual_ref, gain_ref,
    attn_ref, routed_ref, squares_ref,
    wout, gotp, gots, mixed, ysendp, ysends, ygotp, ygots, heads_out, product,
    xbuf, zsend, zbuf, rows_all, sq_all,
    wsem, s1, r1, s2, r2, s3, r3, xs, xr, zs, zr, gs, gr, fs, fr,
):
    c, e, core, z, x, sibling, across, xpeer = places()
    load = pltpu.make_async_copy(wout_hbm, wout, wsem)
    load.start()
    greet()
    half = gotp.shape[0]
    heads = gotp.shape[1] // 128
    pieces = 4
    width = gotp.shape[1] // pieces
    mine, theirs = block_of(core, half), block_of(1 - core, half)
    first = [
        remote(stat_ref.at[theirs, :], gots, s1.at[0], r1.at[0], (sibling, e)),
        remote(part_ref.at[theirs, :], gotp, s1.at[1], r1.at[1], (sibling, e)),
    ]
    for copy in first:
        copy.start()

    def join(own_stat, other_stat):
        lane = lax.broadcasted_iota(jnp.int32, own_stat.shape, 1)
        is_top = lane < heads
        top = jnp.maximum(own_stat, other_stat)
        own_factor = jnp.exp2(jnp.where(is_top, own_stat - top, 0.0))
        other_factor = jnp.exp2(jnp.where(is_top, other_stat - top, 0.0))
        own_wide = pltpu.roll(own_factor, heads, 1)
        other_wide = pltpu.roll(other_factor, heads, 1)
        total = own_stat * own_wide + other_stat * other_wide
        return jnp.where(is_top, top, total), own_factor, other_factor

    first[0].wait_recv()
    stat, own_factor, other_factor = join(stat_ref[mine, :], gots[...])
    ysends[...] = stat
    second_stat = remote(ysends, ygots, s2.at[pieces], r2.at[pieces], (across, e))
    second_stat.start()
    first[1].wait_recv()
    second, third = [], []
    for j in range(pieces):
        for h in range(j * heads // pieces, (j + 1) * heads // pieces):
            at = slice(h * 128, (h + 1) * 128)
            value = part_ref[mine, at].astype(F32) * own_factor[:, h : h + 1]
            value += gotp[:, at].astype(F32) * other_factor[:, h : h + 1]
            mixed[:, at] = value
            ysendp[:, at] = value.astype(BF16)
        at = pl.ds(j * width, width)
        second.append(remote(ysendp.at[:, at], ygotp.at[:, at], s2.at[j], r2.at[j], (across, e)))
        second[j].start()
    second_stat.wait_recv()
    last, own_factor, other_factor = join(stat, ygots[...])
    for j in range(pieces):
        second[j].wait_recv()
        for h in range(j * heads // pieces, (j + 1) * heads // pieces):
            at = slice(h * 128, (h + 1) * 128)
            value = mixed[:, at] * own_factor[:, h : h + 1]
            value += ygotp[:, at].astype(F32) * other_factor[:, h : h + 1]
            heads_out[mine, at] = (value / last[:, heads + h : heads + h + 1]).astype(BF16)
        at = pl.ds(j * width, width)
        third.append(
            remote(heads_out.at[mine, at], heads_out.at[mine, at], s3.at[j], r3.at[j], (sibling, e))
        )
        third[j].start()
    load.wait()
    for copy in third:
        copy.wait_recv()

    columns = product.shape[1]
    span = columns // 2
    spans = [pl.ds(0, span), pl.ds(span, span)]
    start, forward, finish, drain = scatter_sums(
        product, xbuf, zsend, zbuf, xs, xr, zs, zr, spans
    )
    for j in range(2):
        product[:, spans[j]] = jnp.dot(
            heads_out[...], wout[:, spans[j]], preferred_element_type=F32
        ).astype(BF16)
        start(j)
    forward(0)
    forward(1)
    rows = attn_ref.shape[0]
    here = block_of(e, rows)
    squares = jnp.zeros((rows, 1), F32)
    for j in range(2):
        at = spans[j]
        total = finish(j)
        attn_ref[:, at] = total.astype(BF16)
        state = residual_ref[:, at].astype(F32) + total
        rows_all[here, at] = (state * gain_ref[:, at].astype(F32)).astype(BF16)
        squares += jnp.sum(state * state, axis=1, keepdims=True)
    sq_all[here, :] = jnp.broadcast_to(squares, (rows, 128))

    def zcopies(k):
        to = (c, (z + k) % 4 * 2 + x)
        return [
            remote(a.at[here, :], a.at[here, :], gs.at[i, k], gr.at[i, k], to)
            for i, a in enumerate((rows_all, sq_all))
        ]

    def xcopies(k):
        block = block_of((z + 4 - k) % 4 * 2 + x, rows)
        return [
            remote(a.at[block, :], a.at[block, :], fs.at[i, k], fr.at[i, k], (c, xpeer))
            for i, a in enumerate((rows_all, sq_all))
        ]

    for k in (2, 1, 3):
        for copy in zcopies(k):
            copy.start()
    for copy in xcopies(0):
        copy.start()
    for k in (1, 3, 2):
        for copy in zcopies(k):
            copy.wait_recv()
        for copy in xcopies(k):
            copy.start()
    for k in range(4):
        for copy in xcopies(k):
            copy.wait_recv()
    for k in range(4):
        for copy in xcopies(k):
            copy.wait_send()
    for k in (1, 2, 3):
        for copy in zcopies(k):
            copy.wait_send()
    drain()
    for copy in first + second + third + [second_stat]:
        copy.wait_send()
    routed_ref[...] = rows_all[...]
    squares_ref[...] = sq_all[...]


def middle(part, stat, w_out, residual, gain):
    nodes, flat = part.shape
    rows, columns = residual.shape
    half = nodes // 2
    vmem = pl.BlockSpec(memory_space=pltpu.VMEM)
    dma = pltpu.SemaphoreType.DMA
    return pl.pallas_call(
        middle_kernel,
        out_shape=(
            jax.ShapeDtypeStruct((rows, columns), BF16),
            jax.ShapeDtypeStruct((nodes, columns), BF16),
            jax.ShapeDtypeStruct((nodes, 128), F32),
        ),
        in_specs=[vmem, vmem, pl.BlockSpec(memory_space=pl.ANY), vmem, vmem],
        out_specs=(vmem, vmem, vmem),
        scratch_shapes=[
            pltpu.VMEM(w_out.shape, BF16),
            pltpu.VMEM((half, flat), BF16),
            pltpu.VMEM((half, 128), F32),
            pltpu.VMEM((half, flat), F32),
            pltpu.VMEM((half, flat), BF16),
            pltpu.VMEM((half, 128), F32),
            pltpu.VMEM((half, flat), BF16),
            pltpu.VMEM((half, 128), F32),
            pltpu.VMEM((nodes, flat), BF16),
            pltpu.VMEM((nodes, columns), BF16),
            pltpu.VMEM((4, rows, columns), BF16),
            pltpu.VMEM((3, rows, columns), BF16),
            pltpu.VMEM((3, rows, columns), BF16),
            pltpu.VMEM((nodes, columns), BF16),
            pltpu.VMEM((nodes, 128), F32),
            dma, dma((2,)), dma((2,)), dma((5,)), dma((5,)), dma((4,)), dma((4,)),
            dma((2, 4)), dma((2, 4)), dma((2, 3)), dma((2, 3)),
            dma((2, 4)), dma((2, 4)), dma((2, 4)), dma((2, 4)),
        ],
        compiler_params=pltpu.CompilerParams(
            collective_id=1, has_side_effects=True, vmem_limit_bytes=48 * MIB
        ),
        name="middle",
    )(part, stat, w_out, residual, gain)


def expert_kernel(
    routed_ref, squares_ref, placing_ref, weighting_ref, wg_hbm, wu_hbm, wd_hbm,
    moe_ref,
    wgu, wd, chosen, own, send1, got1, send2, got2, hidden, moe, product,
    xbuf, zsend, zbuf, sq_send, sq_got,
    gusem, dsem, s1, r1, s2, r2, s3, r3, qs, qr, xs, xr, zs, zr,
):
    c, e, core, z, x, sibling, across, xpeer = places()
    experts, slots, nodes = placing_ref.shape
    ff = wg_hbm.shape[2]
    half = slots // 2
    mine, theirs = block_of(core, half), block_of(1 - core, half)
    nt = (((1,), (1,)), ((), ()))

    def load_gu(j, slot, i):
        source = (wg_hbm, wu_hbm)[i]
        return pltpu.make_async_copy(source.at[j], wgu.at[slot, i], gusem.at[slot, i])

    def load_d(j):
        return pltpu.make_async_copy(wd_hbm.at[j], wd.at[j], dsem.at[j])

    for j in (0, 1):
        for i in (0, 1):
            load_gu(j, j, i).start()
    greet()
    sq_send[...] = jnp.transpose(squares_ref[...])[:8, :]

    def sq_copy(i):
        to = (sibling, across)[i]
        return remote(sq_send, sq_got.at[i], qs.at[i], qr.at[i], (to, e))

    sq_copy(0).start()

    def copy1(j):
        return remote(send1.at[j], got1.at[j], s1.at[j], r1.at[j], (sibling, e))

    def copy2(j):
        return remote(send2.at[j], got2.at[j], s2.at[j], r2.at[j], (across, e))

    def copy3(j):
        there = hidden.at[j, mine, :]
        return remote(there, there, s3.at[j], r3.at[j], (sibling, e))

    def ins(j, carry):
        slot = j % 2
        chosen[...] = jnp.dot(
            placing_ref[j], routed_ref[...], preferred_element_type=F32
        ).astype(BF16)
        for i in range(2):
            load_gu(j, slot, i).wait()
            own[:, i * ff : (i + 1) * ff] = jnp.dot(
                chosen[...], wgu[slot, i], preferred_element_type=F32
            )
        send1[j] = own[theirs, :].astype(BF16)
        copy1(j).start()

        @pl.when(j + 2 < experts)
        def _():
            for i in (0, 1):
                load_gu(j + 2, slot, i).start()

        @pl.when(j + 2 >= experts)
        def _():
            for d in range(2):
                load_d((j + 2 - experts) * 2 + d).start()

        copy1(j).wait_recv()
        summed = own[mine, :] + got1[j].astype(F32)
        send2[j] = summed.astype(BF16)
        copy2(j).start()
        return carry

    lax.fori_loop(0, experts, ins, 0)
    sq_copy(0).wait_recv()
    sq_copy(0).wait_send()
    sq_send[...] += sq_got[0]
    sq_copy(1).start()
    sq_copy(1).wait_recv()
    square_sum = sq_send[...] + sq_got[1]
    square_high = square_sum.astype(BF16)
    square_low = (square_sum - square_high.astype(F32)).astype(BF16)

    def middle_step(j, carry):
        place = placing_ref[j, mine, :]
        square = lax.dot_general(place, square_high, nt, preferred_element_type=F32)
        square += lax.dot_general(place, square_low, nt, preferred_element_type=F32)
        root = jnp.sqrt(square[:, :1] / D + 1e-06)
        copy2(j).wait_recv()
        total = send2[j].astype(F32) + got2[j].astype(F32)
        gate, up = total[:, :ff] / root, total[:, ff:] / root
        hidden[j, mine, :] = (gate / (1.0 + jnp.exp(-gate)) * up).astype(BF16)
        copy3(j).start()
        return carry

    columns = moe.shape[1]
    span = columns // 2
    spans = [pl.ds(0, span), pl.ds(span, span)]

    def out_step(j, carry):
        copy3(j).wait_recv()
        load_d(j).wait()
        for at in spans:
            answer = jnp.dot(hidden[j], wd[j, :, at], preferred_element_type=F32).astype(BF16)
            add = jnp.dot(weighting_ref[j], answer, preferred_element_type=F32)
            moe[:, at] += add
        return carry

    moe[...] = jnp.zeros_like(moe)
    middle_step(0, 0)

    def both(j, carry):
        out_step(j - 1, 0)
        return middle_step(j, carry)

    lax.fori_loop(1, experts, both, 0)
    start, forward, finish, drain = scatter_sums(
        product, xbuf, zsend, zbuf, xs, xr, zs, zr, spans
    )
    final = experts - 1
    copy3(final).wait_recv()
    load_d(final).wait()
    for i, at in enumerate(spans):
        answer = jnp.dot(hidden[final], wd[final, :, at], preferred_element_type=F32).astype(BF16)
        add = jnp.dot(weighting_ref[final], answer, preferred_element_type=F32)
        product[:, at] = (moe[:, at] + add).astype(BF16)
        start(i)
    forward(0)
    forward(1)
    for j in range(2):
        moe_ref[:, spans[j]] = finish(j).astype(BF16)
    drain()
    sq_copy(1).wait_send()

    def settle(j, carry):
        copy1(j).wait_send()
        copy2(j).wait_send()
        copy3(j).wait_send()
        return carry

    lax.fori_loop(0, experts, settle, 0)


def run_experts(routed, squares, placing, weighting, w_gate, w_up, w_down, rows):
    nodes, columns = routed.shape
    experts, slots, _ = placing.shape
    ff = w_gate.shape[2]
    half = slots // 2
    vmem = pl.BlockSpec(memory_space=pltpu.VMEM)
    hbm = pl.BlockSpec(memory_space=pl.ANY)
    dma = pltpu.SemaphoreType.DMA
    return pl.pallas_call(
        expert_kernel,
        out_shape=jax.ShapeDtypeStruct((rows, columns), BF16),
        in_specs=[vmem] * 4 + [hbm] * 3,
        out_specs=vmem,
        scratch_shapes=[
            pltpu.VMEM((2, 2, columns, ff), BF16),
            pltpu.VMEM((experts, ff, columns), BF16),
            pltpu.VMEM((slots, columns), BF16),
            pltpu.VMEM((slots, 2 * ff), F32),
            pltpu.VMEM((experts, half, 2 * ff), BF16),
            pltpu.VMEM((experts, half, 2 * ff), BF16),
            pltpu.VMEM((experts, half, 2 * ff), BF16),
            pltpu.VMEM((experts, half, 2 * ff), BF16),
            pltpu.VMEM((experts, slots, ff), BF16),
            pltpu.VMEM((nodes, columns), F32),
            pltpu.VMEM((nodes, columns), BF16),
            pltpu.VMEM((4, rows, columns), BF16),
            pltpu.VMEM((3, rows, columns), BF16),
            pltpu.VMEM((3, rows, columns), BF16),
            pltpu.VMEM((8, nodes), F32),
            pltpu.VMEM((2, 8, nodes), F32),
            dma((2, 2)), dma((experts,)),
            dma((experts,)), dma((experts,)), dma((experts,)), dma((experts,)),
            dma((experts,)), dma((experts,)), dma((2,)), dma((2,)),
            dma((2, 4)), dma((2, 4)), dma((2, 3)), dma((2, 3)),
        ],
        compiler_params=pltpu.CompilerParams(
            collective_id=2, has_side_effects=True, vmem_limit_bytes=52 * MIB
        ),
        name="experts",
    )(routed, squares, placing, weighting, w_gate, w_up, w_down)


def slot_tables(routes, route_weights, rows, first, experts_here):
    nodes = routes.shape[0]
    capacity = max(2, 2 * rows * TOPK // EXPERTS)
    slots = nodes // rows * capacity
    hot = routes[:, :, None] == first + jnp.arange(experts_here, dtype=jnp.int32)
    taken = jnp.any(hot, axis=1)
    weight = jnp.sum(jnp.where(hot, route_weights[:, :, None], 0.0), axis=1)
    node = jnp.arange(nodes, dtype=jnp.int32)
    earlier = (node[None, :] < node[:, None]) & (node[None, :] // rows == node[:, None] // rows)
    rank = jnp.dot(
        earlier.astype(BF16), taken.astype(BF16), preferred_element_type=F32
    ).astype(jnp.int32)
    place = jnp.where(taken, (node // rows * capacity)[:, None] + rank, -1).T
    slot = jnp.arange(slots, dtype=jnp.int32)
    placing = (place[:, None, :] == slot[None, :, None]).astype(BF16)
    weighting = jnp.where(
        place[:, :, None] == slot[None, None, :], weight.T[:, :, None], 0.0
    ).astype(BF16)
    return placing, weighting


def kernel_body(
    prompt_cache, tree_latent, parents, query_nope, query_rope, w_absorb, w_value, w_out,
    residual, norm_gain, routes, route_weights, w_gate, w_up, w_down,
):
    nodes = query_nope.shape[0]
    rows = residual.shape[0]
    node = jnp.arange(nodes, dtype=jnp.int32)
    linked = ((parents[:, None] == node[None, :]) | (node[:, None] == node[None, :])).astype(BF16)
    tree_rows = tree_latent.shape[0]
    own_keys = lax.axis_index("ctx") * tree_rows + jnp.arange(tree_rows, dtype=jnp.int32)
    select = (node[:, None] == own_keys[None, :]).astype(BF16)
    experts_here = w_gate.shape[0]
    placing, weighting = slot_tables(
        routes, route_weights, rows, lax.axis_index("exp") * experts_here, experts_here
    )
    part, stat = attention(
        query_nope.reshape(nodes, -1), query_rope.transpose(1, 0, 2),
        w_absorb, w_value, prompt_cache, tree_latent, linked, select,
    )
    attn_out, routed, squares = middle(part, stat, w_out, residual, norm_gain.reshape(1, -1))
    moe_out = run_experts(
        routed, squares, placing, weighting, w_gate, w_up, w_down, rows
    )
    return attn_out, moe_out


def solution(mesh):
    body = kernel_body if (mesh.shape["ctx"], mesh.shape["exp"]) == (4, 8) else plain_body
    placed = (
        P("ctx", None),
        P("ctx", None),
        P(),
        P(None, "exp", None),
        P(None, "exp", None),
        P("exp", None, None),
        P("exp", None, None),
        P("exp", "ctx"),
        P("exp", "ctx"),
        P("ctx"),
        P(),
        P(),
        P("exp", "ctx", None),
        P("exp", "ctx", None),
        P("exp", None, "ctx"),
    )
    return jax.shard_map(
        body,
        mesh=mesh,
        in_specs=placed,
        out_specs=(P("exp", "ctx"), P("exp", "ctx")),
        check_vma=False,
    )
```

```python
import jax
import jax.numpy as jnp
from jax import lax
from jax.experimental import pallas as pl
from jax.experimental.pallas import tpu as pltpu
from jax.sharding import PartitionSpec as P

D = 7168
TOPK = 8
EXPERTS = 32


NEG_FILL = -1e30
EXACT_PRODUCTS = lax.Precision.HIGHEST


def merged(array, axis, join):
    gathered = jax.tree.map(
        lambda a, kind: lax.all_gather(a.astype(kind), axis),
        array,
        (jnp.bfloat16, jnp.bfloat16, jnp.bfloat16),
    )

    def take(source):
        return jax.tree.map(
            lambda a, own: lax.dynamic_index_in_dim(a, source, 0, False).astype(own.dtype),
            gathered,
            array,
        )

    return lax.fori_loop(
        1, lax.axis_size(axis), lambda source, state: join(state, take(source)), take(0)
    )


def ancestry(parents):
    node_total = parents.shape[0]
    linked = (parents[:, None] == jnp.arange(node_total, dtype=jnp.int32)[None, :]).astype(
        jnp.float32
    )
    ancestors = jnp.eye(node_total, dtype=jnp.float32) + linked
    for repeat in range(node_total.bit_length()):
        ancestors = jnp.minimum(jnp.dot(ancestors, ancestors, precision=EXACT_PRODUCTS), 1.0)
    return ancestors


def slot_ranks(routes, block_rows):
    onehot = (routes[:, :, None] == jnp.arange(EXPERTS, dtype=jnp.int32)).astype(jnp.int32)
    grouped = onehot.reshape(-1, block_rows * TOPK, EXPERTS)
    before = jnp.cumsum(grouped, axis=1) - grouped
    return jnp.sum(before * grouped, axis=2).reshape(routes.shape)


def merge_parts(earlier, latter):
    first_top, first_total, first_mix = earlier
    second_top, second_total, second_mix = latter
    top_score = jnp.maximum(first_top, second_top)
    first_factor = jnp.exp(first_top - top_score)
    second_factor = jnp.exp(second_top - top_score)
    weight_total = first_total * first_factor + second_total * second_factor
    combined = first_mix * first_factor[..., None] + second_mix * second_factor[..., None]
    return (top_score, weight_total, combined)


def combine_parts(top_score, weight_total, partial_mix):
    return merged((top_score, weight_total, partial_mix), "ctx", merge_parts)


def expert_block(pieces, w_gate, w_up, w_down):
    blocks, squares = pieces
    gate_part = jnp.einsum("sjkd,jdf->sjkf", blocks, w_gate, preferred_element_type=jnp.float32)
    up_part = jnp.einsum("sjkd,jdf->sjkf", blocks, w_up, preferred_element_type=jnp.float32)
    gate_sum, up_sum, square_sum = (
        lax.psum(gate_part.astype(jnp.bfloat16), "ctx").astype(jnp.float32),
        lax.psum(up_part.astype(jnp.bfloat16), "ctx").astype(jnp.float32),
        lax.psum(squares.astype(jnp.float32).astype(jnp.bfloat16), "ctx").astype(jnp.float32),
    )
    root_mean = jnp.sqrt(square_sum / D + 1e-06)[..., None]
    expert_hidden = (jax.nn.silu(gate_sum / root_mean) * (up_sum / root_mean)).astype(jnp.bfloat16)
    return jnp.einsum(
        "sjkf,jfd->sjkd", expert_hidden, w_down, preferred_element_type=jnp.float32
    ).astype(jnp.bfloat16)


def plain_body(
    prompt_cache,
    tree_latent,
    parents,
    query_nope,
    query_rope,
    w_absorb,
    w_value,
    w_out,
    residual,
    norm_gain,
    routes,
    route_weights,
    w_gate,
    w_up,
    w_down,
):
    node_total, heads_here, nope_width = query_nope.shape
    latent_width = w_absorb.shape[2]
    score_scale = (nope_width + query_rope.shape[2]) ** (-0.5)
    dims_last = (((1,), (1,)), ((), ()))
    absorbed = jnp.einsum(
        "nhc,hcl->nhl", query_nope, w_absorb, preferred_element_type=jnp.float32
    ).astype(jnp.bfloat16)
    queries = jnp.concatenate([absorbed, query_rope], axis=2).reshape(node_total * heads_here, -1)
    tree_rows = tree_latent.shape[0]
    ancestors = ancestry(parents)
    tree_columns = lax.dynamic_slice_in_dim(
        ancestors, lax.axis_index("ctx") * tree_rows, tree_rows, 1
    )
    prompt_scores = lax.dot_general(
        queries, prompt_cache, dims_last, preferred_element_type=jnp.float32
    )
    prompt_scores = prompt_scores.reshape(node_total, heads_here, -1) * score_scale
    tree_scores = lax.dot_general(
        queries, tree_latent, dims_last, preferred_element_type=jnp.float32
    )
    tree_scores = tree_scores.reshape(node_total, heads_here, -1) * score_scale
    tree_scores = jnp.where(tree_columns[:, None, :] > 0.5, tree_scores, NEG_FILL)
    top_score = jnp.maximum(jnp.max(prompt_scores, axis=2), jnp.max(tree_scores, axis=2))
    prompt_exp = jnp.exp(prompt_scores - top_score[..., None])
    tree_exp = jnp.exp(tree_scores - top_score[..., None])
    weight_total = jnp.sum(prompt_exp, axis=2) + jnp.sum(tree_exp, axis=2)
    latent_mix = jnp.dot(
        prompt_exp.reshape(node_total * heads_here, -1).astype(jnp.bfloat16),
        prompt_cache[:, :latent_width],
        preferred_element_type=jnp.float32,
    )
    latent_mix = latent_mix + jnp.dot(
        tree_exp.reshape(node_total * heads_here, -1).astype(jnp.bfloat16),
        tree_latent[:, :latent_width],
        preferred_element_type=jnp.float32,
    )
    latent_mix = latent_mix.reshape(node_total, heads_here, latent_width)
    value_weights = w_value.astype(jnp.float32)
    projected = jnp.einsum("nhl,hlv->nhv", latent_mix, value_weights, precision=EXACT_PRODUCTS)
    top_score, weight_total, projected = combine_parts(top_score, weight_total, projected)
    heads_out = (projected / weight_total[..., None]).astype(jnp.bfloat16).reshape(node_total, -1)
    row_count = residual.shape[0]
    attn_sum = lax.psum_scatter(
        jnp.dot(heads_out, w_out, preferred_element_type=jnp.float32).astype(jnp.bfloat16),
        "exp",
        scatter_dimension=0,
        tiled=True,
    ).astype(jnp.float32)
    state = residual.astype(jnp.float32) + attn_sum
    routed = (state * norm_gain.astype(jnp.float32)).astype(jnp.bfloat16)
    group_squares = jnp.sum(state * state, axis=1).astype(jnp.bfloat16)
    capacity = max(2, 2 * row_count * TOPK // EXPERTS)
    senders = lax.axis_size("exp")
    experts_here = w_gate.shape[0]
    exp_place = lax.axis_index("exp")
    own_routes = lax.dynamic_slice_in_dim(routes, exp_place * row_count, row_count, 0)
    own_weights = lax.dynamic_slice_in_dim(route_weights, exp_place * row_count, row_count, 0)
    slot_rank = slot_ranks(own_routes, row_count)
    expert_hot = (own_routes[:, :, None] == jnp.arange(EXPERTS, dtype=jnp.int32)).astype(
        jnp.float32
    )
    slot_hot = (slot_rank[:, :, None] == jnp.arange(capacity, dtype=jnp.int32)).astype(jnp.float32)
    placing = jnp.einsum("rkx,rks->xsr", expert_hot, slot_hot)
    send_blocks = jnp.einsum(
        "xsr,rd->xsd", placing.astype(jnp.bfloat16), routed, preferred_element_type=jnp.float32
    )
    send_blocks = send_blocks.astype(jnp.bfloat16).reshape(senders, experts_here, capacity, -1)
    send_squares = jnp.einsum(
        "xsr,r->xs", placing, group_squares.astype(jnp.float32), precision=EXACT_PRODUCTS
    )
    send_squares = send_squares.astype(jnp.bfloat16).reshape(senders, experts_here, capacity)
    answers = expert_block(
        (
            lax.all_to_all(send_blocks, "exp", split_axis=0, concat_axis=0, tiled=True),
            lax.all_to_all(send_squares, "exp", split_axis=0, concat_axis=0, tiled=True),
        ),
        w_gate,
        w_up,
        w_down,
    )
    returned = lax.all_to_all(answers, "exp", split_axis=0, concat_axis=0, tiled=True)
    returned = returned.reshape(EXPERTS, capacity, -1).astype(jnp.float32)
    weighting = jnp.einsum(
        "rkx,rks,rk->rxs", expert_hot, slot_hot, own_weights, precision=EXACT_PRODUCTS
    )
    moe_sum = jnp.einsum("rxs,xsd->rd", weighting, returned, precision=EXACT_PRODUCTS)
    return (attn_sum.astype(jnp.bfloat16), moe_sum.astype(jnp.bfloat16))


LOG2E = 1.4426950408889634
MESH = pl.DeviceIdType.MESH
MIB = 1024 * 1024
F32 = jnp.float32
BF16 = jnp.bfloat16
HEADS_PER_STEP = 2


def attention_kernel(
    scale, qn_ref, qr_ref, wabs_ref, wval_ref, cache_ref, tree_ref, linked_ref, select_ref,
    part_ref, stat_ref, visible,
):
    step = pl.program_id(0)
    nodes = qn_ref.shape[0]
    latent = wabs_ref.shape[2]
    nope = wabs_ref.shape[1]
    vdim = wval_ref.shape[2]
    heads = pl.num_programs(0) * HEADS_PER_STEP

    @pl.when(step == 0)
    def _():
        reach = linked_ref[...]
        for _ in range((nodes - 1).bit_length()):
            reach = jnp.minimum(jnp.dot(reach, reach, preferred_element_type=F32), 1.0).astype(BF16)
        visible[...] = jnp.dot(reach, select_ref[...], preferred_element_type=F32)
        stat_ref[...] = jnp.zeros_like(stat_ref)

    nt = (((1,), (1,)), ((), ()))
    factor = scale * LOG2E
    queries = jnp.concatenate(
        [
            jnp.concatenate(
                [
                    jnp.dot(
                        qn_ref[:, h * nope : (h + 1) * nope], wabs_ref[h],
                        preferred_element_type=F32,
                    ).astype(BF16),
                    jnp.transpose(qr_ref[h].astype(F32)).astype(BF16),
                ],
                axis=1,
            )
            for h in range(HEADS_PER_STEP)
        ],
        axis=0,
    )
    keys = cache_ref.shape[1]
    chunk = 512
    scores = [
        jnp.dot(queries, cache_ref[:, at : at + chunk], preferred_element_type=F32) * factor
        for at in range(0, keys, chunk)
    ]
    tree_scores = lax.dot_general(queries, tree_ref[...], nt, preferred_element_type=F32) * factor
    seen = jnp.concatenate([visible[...]] * HEADS_PER_STEP, axis=0)
    tree_scores = jnp.where(seen > 0.5, tree_scores, NEG_FILL)
    highest = scores[0]
    for piece in scores[1:]:
        highest = jnp.maximum(highest, piece)
    top = jnp.maximum(
        jnp.max(highest, axis=1, keepdims=True), jnp.max(tree_scores, axis=1, keepdims=True)
    )
    tree_exp = jnp.exp2(tree_scores - top)
    total = jnp.sum(tree_exp, axis=1, keepdims=True)
    mix = jnp.dot(tree_exp.astype(BF16), tree_ref[:, :latent], preferred_element_type=F32)
    sums = None
    for i, piece in enumerate(scores):
        weight = jnp.exp2(piece - top)
        sums = weight if sums is None else sums + weight
        mix += lax.dot_general(
            weight.astype(BF16), cache_ref[:latent, i * chunk : (i + 1) * chunk], nt,
            preferred_element_type=F32,
        )
    total += jnp.sum(sums, axis=1, keepdims=True)
    lane = lax.broadcasted_iota(jnp.int32, stat_ref.shape, 1)
    stat = stat_ref[...]
    for h in range(HEADS_PER_STEP):
        rows = slice(h * nodes, (h + 1) * nodes)
        head = step * HEADS_PER_STEP + h
        part_ref[:, h * vdim : (h + 1) * vdim] = jnp.dot(
            mix[rows].astype(BF16), wval_ref[h], preferred_element_type=F32
        ).astype(BF16)
        stat = jnp.where(lane == head, top[rows], stat)
        stat = jnp.where(lane == heads + head, total[rows], stat)
    stat_ref[...] = stat


def attention(qn, qr, wabs, wval, cache, tree, linked, select):
    nodes = qn.shape[0]
    heads, nope, latent = wabs.shape
    vdim = wval.shape[2]
    rope = qr.shape[1]
    per = HEADS_PER_STEP
    whole = lambda a: pl.BlockSpec(a.shape, lambda i: (0,) * a.ndim)
    scale = float((nope + rope) ** (-0.5))

    def kernel(*refs):
        attention_kernel(scale, *refs)

    return pl.pallas_call(
        kernel,
        grid=(heads // per,),
        out_shape=(
            jax.ShapeDtypeStruct((nodes, heads * vdim), BF16),
            jax.ShapeDtypeStruct((nodes, 128), F32),
        ),
        in_specs=[
            pl.BlockSpec((nodes, per * nope), lambda i: (0, i)),
            pl.BlockSpec((per, rope, nodes), lambda i: (i, 0, 0)),
            pl.BlockSpec((per, nope, latent), lambda i: (i, 0, 0)),
            pl.BlockSpec((per, latent, vdim), lambda i: (i, 0, 0)),
            whole(cache), whole(tree), whole(linked), whole(select),
        ],
        out_specs=(
            pl.BlockSpec((nodes, per * vdim), lambda i: (0, i)),
            pl.BlockSpec((nodes, 128), lambda i: (0, 0)),
        ),
        scratch_shapes=[pltpu.VMEM((nodes, tree.shape[0]), F32)],
        compiler_params=pltpu.CompilerParams(
            dimension_semantics=("arbitrary",), vmem_limit_bytes=48 * MIB
        ),
        name="attention",
    )(qn, qr, wabs, wval, cache, tree, linked, select)


def places():
    c = lax.axis_index("ctx")
    e = lax.axis_index("exp")
    core, z, x = c % 2, e // 2, e % 2
    return c, e, core, z, x, c + 1 - 2 * core, c + 2 - 4 * (c // 2), e + 1 - 2 * x


def greet():
    c, e, core, z, x, sibling, across, xpeer = places()
    barrier = pltpu.get_barrier_semaphore()
    peers = [(sibling, e), (across, e), (c, xpeer)]
    peers += [(c, (z + k) % 4 * 2 + x) for k in (1, 2, 3)]
    for peer in peers:
        pl.semaphore_signal(barrier, inc=1, device_id=peer, device_id_type=MESH)
    pl.semaphore_wait(barrier, len(peers))


def remote(src, dst, send, recv, to):
    return pltpu.make_async_remote_copy(
        src_ref=src, dst_ref=dst, send_sem=send, recv_sem=recv, device_id=to, device_id_type=MESH
    )


def block_of(index, rows):
    return pl.ds(pl.multiple_of(index * rows, rows), rows)


def scatter_sums(part, xbuf, zsend, zbuf, xs, xr, zs, zr, spans):
    c, e, core, z, x, sibling, across, xpeer = places()
    rows = zsend.shape[1]

    def xcopy(j, k):
        at, zt = spans[j], (z + k) % 4
        return remote(
            part.at[block_of(zt * 2 + 1 - x, rows), at], xbuf.at[k, :, at],
            xs.at[j, k], xr.at[j, k], (c, xpeer),
        )

    def zcopy(j, k):
        at = spans[j]
        return remote(
            zsend.at[k - 1, :, at], zbuf.at[k - 1, :, at],
            zs.at[j, k - 1], zr.at[j, k - 1], (c, (z + k) % 4 * 2 + x),
        )

    def start(j):
        for k in (2, 1, 3, 0):
            xcopy(j, k).start()

    def forward(j):
        at = spans[j]
        for k in (2, 1, 3):
            xcopy(j, k).wait_recv()
            own = part[block_of((z + k) % 4 * 2 + x, rows), at].astype(F32)
            zsend[k - 1, :, at] = (own + xbuf[k, :, at].astype(F32)).astype(BF16)
            zcopy(j, k).start()

    def finish(j):
        at = spans[j]
        xcopy(j, 0).wait_recv()
        total = part[block_of(e, rows), at].astype(F32) + xbuf[0, :, at].astype(F32)
        for k in (1, 3, 2):
            zcopy(j, k).wait_recv()
            total += zbuf[k - 1, :, at].astype(F32)
        return total

    def drain():
        for j in range(len(spans)):
            for k in range(4):
                xcopy(j, k).wait_send()
            for k in (1, 2, 3):
                zcopy(j, k).wait_send()

    return start, forward, finish, drain


def middle_kernel(
    part_ref, stat_ref, wout_hbm, residual_ref, gain_ref,
    attn_ref, routed_ref, squares_ref,
    wout, gotp, gots, mixed, ysendp, ysends, ygotp, ygots, heads_out, product,
    xbuf, zsend, zbuf, rows_all, sq_all,
    wsem, s1, r1, s2, r2, s3, r3, xs, xr, zs, zr, gs, gr, fs, fr,
):
    c, e, core, z, x, sibling, across, xpeer = places()
    load = pltpu.make_async_copy(wout_hbm, wout, wsem)
    load.start()
    greet()
    half = gotp.shape[0]
    heads = gotp.shape[1] // 128
    pieces = 4
    width = gotp.shape[1] // pieces
    mine, theirs = block_of(core, half), block_of(1 - core, half)
    first = [
        remote(stat_ref.at[theirs, :], gots, s1.at[0], r1.at[0], (sibling, e)),
        remote(part_ref.at[theirs, :], gotp, s1.at[1], r1.at[1], (sibling, e)),
    ]
    for copy in first:
        copy.start()

    def join(own_stat, other_stat):
        lane = lax.broadcasted_iota(jnp.int32, own_stat.shape, 1)
        is_top = lane < heads
        top = jnp.maximum(own_stat, other_stat)
        own_factor = jnp.exp2(jnp.where(is_top, own_stat - top, 0.0))
        other_factor = jnp.exp2(jnp.where(is_top, other_stat - top, 0.0))
        own_wide = pltpu.roll(own_factor, heads, 1)
        other_wide = pltpu.roll(other_factor, heads, 1)
        total = own_stat * own_wide + other_stat * other_wide
        return jnp.where(is_top, top, total), own_factor, other_factor

    first[0].wait_recv()
    stat, own_factor, other_factor = join(stat_ref[mine, :], gots[...])
    ysends[...] = stat
    second_stat = remote(ysends, ygots, s2.at[pieces], r2.at[pieces], (across, e))
    second_stat.start()
    first[1].wait_recv()
    second, third = [], []
    for j in range(pieces):
        for h in range(j * heads // pieces, (j + 1) * heads // pieces):
            at = slice(h * 128, (h + 1) * 128)
            value = part_ref[mine, at].astype(F32) * own_factor[:, h : h + 1]
            value += gotp[:, at].astype(F32) * other_factor[:, h : h + 1]
            mixed[:, at] = value
            ysendp[:, at] = value.astype(BF16)
        at = pl.ds(j * width, width)
        second.append(remote(ysendp.at[:, at], ygotp.at[:, at], s2.at[j], r2.at[j], (across, e)))
        second[j].start()
    second_stat.wait_recv()
    last, own_factor, other_factor = join(stat, ygots[...])
    for j in range(pieces):
        second[j].wait_recv()
        for h in range(j * heads // pieces, (j + 1) * heads // pieces):
            at = slice(h * 128, (h + 1) * 128)
            value = mixed[:, at] * own_factor[:, h : h + 1]
            value += ygotp[:, at].astype(F32) * other_factor[:, h : h + 1]
            heads_out[mine, at] = (value / last[:, heads + h : heads + h + 1]).astype(BF16)
        at = pl.ds(j * width, width)
        third.append(
            remote(heads_out.at[mine, at], heads_out.at[mine, at], s3.at[j], r3.at[j], (sibling, e))
        )
        third[j].start()
    load.wait()
    for copy in third:
        copy.wait_recv()

    columns = product.shape[1]
    span = columns // 2
    spans = [pl.ds(0, span), pl.ds(span, span)]
    start, forward, finish, drain = scatter_sums(
        product, xbuf, zsend, zbuf, xs, xr, zs, zr, spans
    )
    for j in range(2):
        product[:, spans[j]] = jnp.dot(
            heads_out[...], wout[:, spans[j]], preferred_element_type=F32
        ).astype(BF16)
        start(j)
    forward(0)
    forward(1)
    rows = attn_ref.shape[0]
    here = block_of(e, rows)
    squares = jnp.zeros((rows, 1), F32)
    for j in range(2):
        at = spans[j]
        total = finish(j)
        attn_ref[:, at] = total.astype(BF16)
        state = residual_ref[:, at].astype(F32) + total
        rows_all[here, at] = (state * gain_ref[:, at].astype(F32)).astype(BF16)
        squares += jnp.sum(state * state, axis=1, keepdims=True)
    sq_all[here, :] = jnp.broadcast_to(squares, (rows, 128))

    def zcopies(k):
        to = (c, (z + k) % 4 * 2 + x)
        return [
            remote(a.at[here, :], a.at[here, :], gs.at[i, k], gr.at[i, k], to)
            for i, a in enumerate((rows_all, sq_all))
        ]

    def xcopies(k):
        block = block_of((z + 4 - k) % 4 * 2 + x, rows)
        return [
            remote(a.at[block, :], a.at[block, :], fs.at[i, k], fr.at[i, k], (c, xpeer))
            for i, a in enumerate((rows_all, sq_all))
        ]

    for k in (2, 1, 3):
        for copy in zcopies(k):
            copy.start()
    for copy in xcopies(0):
        copy.start()
    for k in (1, 3, 2):
        for copy in zcopies(k):
            copy.wait_recv()
        for copy in xcopies(k):
            copy.start()
    for k in range(4):
        for copy in xcopies(k):
            copy.wait_recv()
    for k in range(4):
        for copy in xcopies(k):
            copy.wait_send()
    for k in (1, 2, 3):
        for copy in zcopies(k):
            copy.wait_send()
    drain()
    for copy in first + second + third + [second_stat]:
        copy.wait_send()
    routed_ref[...] = rows_all[...]
    squares_ref[...] = sq_all[...]


def middle(part, stat, w_out, residual, gain):
    nodes, flat = part.shape
    rows, columns = residual.shape
    half = nodes // 2
    vmem = pl.BlockSpec(memory_space=pltpu.VMEM)
    dma = pltpu.SemaphoreType.DMA
    return pl.pallas_call(
        middle_kernel,
        out_shape=(
            jax.ShapeDtypeStruct((rows, columns), BF16),
            jax.ShapeDtypeStruct((nodes, columns), BF16),
            jax.ShapeDtypeStruct((nodes, 128), F32),
        ),
        in_specs=[vmem, vmem, pl.BlockSpec(memory_space=pl.ANY), vmem, vmem],
        out_specs=(vmem, vmem, vmem),
        scratch_shapes=[
            pltpu.VMEM(w_out.shape, BF16),
            pltpu.VMEM((half, flat), BF16),
            pltpu.VMEM((half, 128), F32),
            pltpu.VMEM((half, flat), F32),
            pltpu.VMEM((half, flat), BF16),
            pltpu.VMEM((half, 128), F32),
            pltpu.VMEM((half, flat), BF16),
            pltpu.VMEM((half, 128), F32),
            pltpu.VMEM((nodes, flat), BF16),
            pltpu.VMEM((nodes, columns), BF16),
            pltpu.VMEM((4, rows, columns), BF16),
            pltpu.VMEM((3, rows, columns), BF16),
            pltpu.VMEM((3, rows, columns), BF16),
            pltpu.VMEM((nodes, columns), BF16),
            pltpu.VMEM((nodes, 128), F32),
            dma, dma((2,)), dma((2,)), dma((5,)), dma((5,)), dma((4,)), dma((4,)),
            dma((2, 4)), dma((2, 4)), dma((2, 3)), dma((2, 3)),
            dma((2, 4)), dma((2, 4)), dma((2, 4)), dma((2, 4)),
        ],
        compiler_params=pltpu.CompilerParams(
            collective_id=1, has_side_effects=True, vmem_limit_bytes=48 * MIB
        ),
        name="middle",
    )(part, stat, w_out, residual, gain)


def expert_kernel(
    routed_ref, squares_ref, placing_ref, weighting_ref, wg_hbm, wu_hbm, wd_hbm,
    moe_ref,
    wgu, wd, chosen, own, send1, got1, send2, got2, hidden, moe, product,
    xbuf, zsend, zbuf, sq_send, sq_got,
    gusem, dsem, s1, r1, s2, r2, s3, r3, qs, qr, xs, xr, zs, zr,
):
    c, e, core, z, x, sibling, across, xpeer = places()
    experts, slots, nodes = placing_ref.shape
    ff = wg_hbm.shape[2]
    half = slots // 2
    mine, theirs = block_of(core, half), block_of(1 - core, half)
    nt = (((1,), (1,)), ((), ()))

    def load_gu(j, slot, i):
        source = (wg_hbm, wu_hbm)[i]
        return pltpu.make_async_copy(source.at[j], wgu.at[slot, i], gusem.at[slot, i])

    def load_d(j):
        return pltpu.make_async_copy(wd_hbm.at[j], wd.at[j], dsem.at[j])

    for j in (0, 1):
        for i in (0, 1):
            load_gu(j, j, i).start()
    greet()
    sq_send[...] = jnp.transpose(squares_ref[...])[:8, :]

    def sq_copy(i):
        to = (sibling, across)[i]
        return remote(sq_send, sq_got.at[i], qs.at[i], qr.at[i], (to, e))

    sq_copy(0).start()

    def copy1(j, i):
        at = pl.ds(i * ff, ff)
        return remote(
            send1.at[j, :, at], got1.at[j, :, at], s1.at[j, i], r1.at[j, i], (sibling, e)
        )

    def copy2(j, i):
        at = pl.ds(i * ff, ff)
        return remote(
            send2.at[j, :, at], got2.at[j, :, at], s2.at[j, i], r2.at[j, i], (across, e)
        )

    def copy3(j):
        there = hidden.at[j, mine, :]
        return remote(there, there, s3.at[j], r3.at[j], (sibling, e))

    def merge(j, i):
        at = pl.ds(i * ff, ff)
        copy1(j, i).wait_recv()
        send2[j, :, at] = (own[i, mine, :] + got1[j, :, at].astype(F32)).astype(BF16)
        copy2(j, i).start()

    sq_copy(0).wait_recv()
    sq_copy(0).wait_send()
    sq_send[...] += sq_got[0]
    sq_copy(1).start()

    def ins(j, carry):
        slot = j % 2
        chosen[...] = jnp.dot(
            placing_ref[j], routed_ref[...], preferred_element_type=F32
        ).astype(BF16)
        for i in (0, 1):
            load_gu(j, slot, i).wait()
            own[i] = jnp.dot(chosen[...], wgu[slot, i], preferred_element_type=F32)
            send1[j, :, pl.ds(i * ff, ff)] = own[i, theirs, :].astype(BF16)
            copy1(j, i).start()

            @pl.when(j + 2 < experts)
            def _():
                load_gu(j + 2, slot, i).start()

            @pl.when(j + 2 >= experts)
            def _():
                load_d((j + 2 - experts) * 2 + i).start()

            if i == 0:

                @pl.when(j > 0)
                def _():
                    merge(j - 1, 1)

            else:
                merge(j, 0)
        return carry

    lax.fori_loop(0, experts, ins, 0)
    merge(experts - 1, 1)
    sq_copy(1).wait_recv()
    square_sum = sq_send[...] + sq_got[1]
    square_high = square_sum.astype(BF16)
    square_low = (square_sum - square_high.astype(F32)).astype(BF16)

    def middle_step(j, carry):
        place = placing_ref[j, mine, :]
        square = lax.dot_general(place, square_high, nt, preferred_element_type=F32)
        square += lax.dot_general(place, square_low, nt, preferred_element_type=F32)
        root = jnp.sqrt(square[:, :1] / D + 1e-06)
        copy2(j, 0).wait_recv()
        copy2(j, 1).wait_recv()
        total = send2[j].astype(F32) + got2[j].astype(F32)
        gate, up = total[:, :ff] / root, total[:, ff:] / root
        hidden[j, mine, :] = (gate / (1.0 + jnp.exp(-gate)) * up).astype(BF16)
        copy3(j).start()
        return carry

    columns = moe.shape[1]
    span = columns // 2
    spans = [pl.ds(0, span), pl.ds(span, span)]

    def out_step(j, carry):
        copy3(j).wait_recv()
        load_d(j).wait()
        for at in spans:
            answer = jnp.dot(hidden[j], wd[j, :, at], preferred_element_type=F32).astype(BF16)
            add = jnp.dot(weighting_ref[j], answer, preferred_element_type=F32)
            moe[:, at] += add
        return carry

    moe[...] = jnp.zeros_like(moe)
    middle_step(0, 0)

    def both(j, carry):
        out_step(j - 1, 0)
        return middle_step(j, carry)

    lax.fori_loop(1, experts, both, 0)
    start, forward, finish, drain = scatter_sums(
        product, xbuf, zsend, zbuf, xs, xr, zs, zr, spans
    )
    final = experts - 1
    copy3(final).wait_recv()
    load_d(final).wait()
    for i, at in enumerate(spans):
        answer = jnp.dot(hidden[final], wd[final, :, at], preferred_element_type=F32).astype(BF16)
        add = jnp.dot(weighting_ref[final], answer, preferred_element_type=F32)
        product[:, at] = (moe[:, at] + add).astype(BF16)
        start(i)
    forward(0)
    forward(1)
    for j in range(2):
        moe_ref[:, spans[j]] = finish(j).astype(BF16)
    drain()
    sq_copy(1).wait_send()

    def settle(j, carry):
        for i in (0, 1):
            copy1(j, i).wait_send()
            copy2(j, i).wait_send()
        copy3(j).wait_send()
        return carry

    lax.fori_loop(0, experts, settle, 0)


def run_experts(routed, squares, placing, weighting, w_gate, w_up, w_down, rows):
    nodes, columns = routed.shape
    experts, slots, _ = placing.shape
    ff = w_gate.shape[2]
    half = slots // 2
    vmem = pl.BlockSpec(memory_space=pltpu.VMEM)
    hbm = pl.BlockSpec(memory_space=pl.ANY)
    dma = pltpu.SemaphoreType.DMA
    return pl.pallas_call(
        expert_kernel,
        out_shape=jax.ShapeDtypeStruct((rows, columns), BF16),
        in_specs=[vmem] * 4 + [hbm] * 3,
        out_specs=vmem,
        scratch_shapes=[
            pltpu.VMEM((2, 2, columns, ff), BF16),
            pltpu.VMEM((experts, ff, columns), BF16),
            pltpu.VMEM((slots, columns), BF16),
            pltpu.VMEM((2, slots, ff), F32),
            pltpu.VMEM((experts, half, 2 * ff), BF16),
            pltpu.VMEM((experts, half, 2 * ff), BF16),
            pltpu.VMEM((experts, half, 2 * ff), BF16),
            pltpu.VMEM((experts, half, 2 * ff), BF16),
            pltpu.VMEM((experts, slots, ff), BF16),
            pltpu.VMEM((nodes, columns), F32),
            pltpu.VMEM((nodes, columns), BF16),
            pltpu.VMEM((4, rows, columns), BF16),
            pltpu.VMEM((3, rows, columns), BF16),
            pltpu.VMEM((3, rows, columns), BF16),
            pltpu.VMEM((8, nodes), F32),
            pltpu.VMEM((2, 8, nodes), F32),
            dma((2, 2)), dma((experts,)),
            dma((experts, 2)), dma((experts, 2)), dma((experts, 2)), dma((experts, 2)),
            dma((experts,)), dma((experts,)), dma((2,)), dma((2,)),
            dma((2, 4)), dma((2, 4)), dma((2, 3)), dma((2, 3)),
        ],
        compiler_params=pltpu.CompilerParams(
            collective_id=2, has_side_effects=True, vmem_limit_bytes=52 * MIB
        ),
        name="experts",
    )(routed, squares, placing, weighting, w_gate, w_up, w_down)


def slot_tables(routes, route_weights, rows, first, experts_here):
    nodes = routes.shape[0]
    capacity = max(2, 2 * rows * TOPK // EXPERTS)
    slots = nodes // rows * capacity
    hot = routes[:, :, None] == first + jnp.arange(experts_here, dtype=jnp.int32)
    taken = jnp.any(hot, axis=1)
    weight = jnp.sum(jnp.where(hot, route_weights[:, :, None], 0.0), axis=1)
    node = jnp.arange(nodes, dtype=jnp.int32)
    earlier = (node[None, :] < node[:, None]) & (node[None, :] // rows == node[:, None] // rows)
    rank = jnp.dot(
        earlier.astype(BF16), taken.astype(BF16), preferred_element_type=F32
    ).astype(jnp.int32)
    place = jnp.where(taken, (node // rows * capacity)[:, None] + rank, -1).T
    slot = jnp.arange(slots, dtype=jnp.int32)
    placing = (place[:, None, :] == slot[None, :, None]).astype(BF16)
    weighting = jnp.where(
        place[:, :, None] == slot[None, None, :], weight.T[:, :, None], 0.0
    ).astype(BF16)
    return placing, weighting


def kernel_body(
    prompt_cache, tree_latent, parents, query_nope, query_rope, w_absorb, w_value, w_out,
    residual, norm_gain, routes, route_weights, w_gate, w_up, w_down,
):
    nodes = query_nope.shape[0]
    rows = residual.shape[0]
    node = jnp.arange(nodes, dtype=jnp.int32)
    linked = ((parents[:, None] == node[None, :]) | (node[:, None] == node[None, :])).astype(BF16)
    tree_rows = tree_latent.shape[0]
    own_keys = lax.axis_index("ctx") * tree_rows + jnp.arange(tree_rows, dtype=jnp.int32)
    select = (node[:, None] == own_keys[None, :]).astype(BF16)
    experts_here = w_gate.shape[0]
    placing, weighting = slot_tables(
        routes, route_weights, rows, lax.axis_index("exp") * experts_here, experts_here
    )
    part, stat = attention(
        query_nope.reshape(nodes, -1), query_rope.transpose(1, 2, 0),
        w_absorb, w_value, prompt_cache.T, tree_latent, linked, select,
    )
    attn_out, routed, squares = middle(part, stat, w_out, residual, norm_gain.reshape(1, -1))
    moe_out = run_experts(
        routed, squares, placing, weighting, w_gate, w_up, w_down, rows
    )
    return attn_out, moe_out


def solution(mesh):
    body = kernel_body if (mesh.shape["ctx"], mesh.shape["exp"]) == (4, 8) else plain_body
    placed = (
        P("ctx", None),
        P("ctx", None),
        P(),
        P(None, "exp", None),
        P(None, "exp", None),
        P("exp", None, None),
        P("exp", None, None),
        P("exp", "ctx"),
        P("exp", "ctx"),
        P("ctx"),
        P(),
        P(),
        P("exp", "ctx", None),
        P("exp", "ctx", None),
        P("exp", None, "ctx"),
    )
    return jax.shard_map(
        body,
        mesh=mesh,
        in_specs=placed,
        out_specs=(P("exp", "ctx"), P("exp", "ctx")),
        check_vma=False,
    )
```
